32 devices in a mesh: group: 4 (over z), dev: 8 (over y, x, core).
Axes of the slice: x: 2, y: 2, z: 4, core: 2. Of those that a mesh axis runs over, the one named last changes fastest.
Arguments:
- tokens: bfloat16 [4096, 3584], P(('group', 'dev')), may hold values from -1.5 to 1.5
- out_grad: bfloat16 [4096, 3584], P(('group', 'dev')), may hold values from -0.59765625 to 0.59765625
- gate_weights: bfloat16 [4096, 8], P(('group', 'dev')), may hold values from 0.099609375 to 1
- expert_ids: int32 [4096, 8], P(('group', 'dev')), may hold values from 0 to 31, as said below
- slot_ids: int32 [4096, 8], P(('group', 'dev')), may hold values from 0 to 39, as said below
- up_weight: bfloat16 [32, 3584, 1024], P(('group', 'dev')), may hold values from -0.40039062 to 0.40039062
- down_weight: bfloat16 [32, 1024, 3584], P(('group', 'dev')), may hold values from -0.1875 to 0.1875
Outputs:
- token_grad: bfloat16 [4096, 3584], P(('group', 'dev'))
- gate_grad: bfloat16 [4096, 8], P(('group', 'dev'))
The draws below stay inside these ranges and needn't reach their ends.
Inputs may be any that keep to these rules, and one draw needn't show every extreme that they name: `expert_ids`: expert e lies in group e // 8 and on the device of index e along group+dev. Each token names 8 different experts, 4 in each of exactly 2 groups. In the rows of one device no expert is named more than 40 times and some expert exactly 40 times; no group is named by more than 80 rows and some group by exactly 80. `slot_ids`: in the rows of one device, two entries that name the same expert have different slots.
All inputs are finite; a program needn't handle non-finite values.
Results may differ from the reference program's by a relative error of at most 0.009.
Values may be sent and summed in bfloat16 or wider, within the bound.
A program may use at most 192 MiB of HBM per device.

```python
import math
import jax
import jax.numpy as jnp
from jax import lax

D = 3584
H = 1024
TOPK = 8
TOK_DEV = 128
GROUPS = 4
EXP_GROUP = 8
EXPERTS = 32
TOKENS = 4096
EPG = 4
MOST = 40
GROUP_ROWS = 80
DEVICES = 32


def route_tables(key):
    key = jax.random.fold_in(key, 11)
    key_list = jax.random.split(key, 4)
    blocks = TOKENS // TOK_DEV
    home_group = jax.random.randint(key_list[0], (blocks, 1), 0, GROUPS)
    token_order = jnp.argsort(jax.random.randint(key_list[1], (blocks, TOK_DEV), 0, 1 << 20) * TOK_DEV + jnp.arange(TOK_DEV), axis=1)
    token_rank = jnp.argsort(token_order, axis=1)
    rank_pos = jnp.arange(TOK_DEV)[None, :]
    other_count = GROUPS - 1
    with_home = rank_pos < GROUP_ROWS
    rotation = (rank_pos - GROUP_ROWS) % other_count
    group_one = jnp.where(with_home, home_group, (home_group + 1 + rotation) % GROUPS)
    group_two = jnp.where(with_home, (home_group + 1 + rank_pos % other_count) % GROUPS, (home_group + 1 + (rotation + 1) % other_count) % GROUPS)
    group_ids = jnp.arange(GROUPS)
    names_group = ((group_one[:, :, None] == group_ids) | (group_two[:, :, None] == group_ids)).astype(jnp.int32)
    group_rank = jnp.cumsum(names_group, axis=1) - 1
    expert_order = jnp.argsort(jax.random.randint(key_list[2], (blocks, GROUPS, EXP_GROUP), 0, 1 << 20) * EXP_GROUP + jnp.arange(EXP_GROUP), axis=2)
    pick_off = jnp.arange(EPG)[None, None, :]
    block_ids = jnp.arange(blocks)[:, None]

    def picks(chosen):
        order_pos = jnp.take_along_axis(group_rank, chosen[:, :, None], axis=2)
        pick_pos = order_pos * EPG + pick_off
        members = expert_order[block_ids, chosen]
        local_ids = jnp.take_along_axis(members, pick_pos % EXP_GROUP, axis=2)
        return (chosen[:, :, None] * EXP_GROUP + local_ids, pick_pos // EXP_GROUP)
    ids_one, slot_one = picks(group_one)
    ids_two, slot_two = picks(group_two)
    ids_rank = jnp.concatenate([ids_one, ids_two], axis=2)
    slot_rank = jnp.concatenate([slot_one, slot_two], axis=2)
    entry_order = jnp.argsort(jax.random.randint(key_list[3], (blocks, TOK_DEV, TOPK), 0, 1 << 20) * TOPK + jnp.arange(TOPK), axis=2)
    ids_rank = jnp.take_along_axis(ids_rank, entry_order, axis=2)
    slot_rank = jnp.take_along_axis(slot_rank, entry_order, axis=2)
    ids_token = jnp.take_along_axis(ids_rank, token_rank[:, :, None], axis=1)
    slot_token = jnp.take_along_axis(slot_rank, token_rank[:, :, None], axis=1)
    return (ids_token.reshape(TOKENS, TOPK).astype(jnp.int32), slot_token.reshape(TOKENS, TOPK).astype(jnp.int32))


def draw_expert_ids(key, part):
    return route_tables(key)[0]


def draw_slot_ids(key, part):
    return route_tables(key)[1]


def steps_of(own_key, extent, pieces, least, largest):
    def one(dim, shards_of):
        heights = jax.random.uniform(jax.random.fold_in(jax.random.fold_in(own_key, 6), dim), (shards_of,), jnp.float32, least / len(pieces), largest / len(pieces))
        return jnp.repeat(jnp.exp(heights), extent[dim] // shards_of).reshape((-1,) + (1,) * (len(extent) - dim - 1))

    level = one(*pieces[0])
    for cut in pieces[1:]:
        level = level * one(*cut)
    return level


def bell_draw(own_key, extent, deviation, limit, cuts=(), held_as=jnp.bfloat16):
    values = deviation * jax.random.normal(own_key, extent, jnp.float32)
    if cuts:
        values = values * steps_of(own_key, extent, cuts, -0.22, 0.18)
    return jnp.clip(values, -limit, limit).astype(held_as)


def setup_inputs(seed: int = 0) -> dict:
    keys = jax.random.split(jax.random.key(seed), 8)
    tokens = bell_draw(keys[0], (TOKENS, D), 0.25, 1.5, ((0, 32),))
    out_grad = bell_draw(keys[1], (TOKENS, D), 0.1, 0.59765625, ((0, 32),))
    gate_weights = jnp.clip(jnp.exp(math.log(1.0) - 2.306499 * jax.random.uniform(keys[2], (TOKENS, TOPK), jnp.float32) ** steps_of(keys[2], (TOKENS, TOPK), ((0, 32),), -0.2, 0.2)), 0.099609375, 1.0).astype(jnp.bfloat16)
    expert_ids = draw_expert_ids(jax.random.fold_in(keys[7], 71), 0)
    slot_ids = draw_slot_ids(jax.random.fold_in(keys[7], 71), 0)
    up_weight = bell_draw(keys[5], (EXPERTS, D, H), (4.0 / D ** 0.5), 0.40039062, ((0, 32),))
    down_weight = bell_draw(keys[6], (EXPERTS, H, D), H ** -0.5, 0.1875, ((0, 32),))
    return dict(tokens=tokens, out_grad=out_grad, gate_weights=gate_weights, expert_ids=expert_ids, slot_ids=slot_ids, up_weight=up_weight, down_weight=down_weight)


def silu_slope(values):
    sigmoid_up = jax.nn.sigmoid(values)
    return sigmoid_up * (1.0 + values * (1.0 - sigmoid_up))


def expert_rows(token_rows, grad_rows, gate_rows, up_matrix, down_matrix):
    raised = jnp.dot(token_rows, up_matrix, preferred_element_type=jnp.float32)
    backward = lax.dot_general(grad_rows, down_matrix, (((1,), (1,)), ((), ())), preferred_element_type=jnp.float32)
    gate_grad = jnp.sum(jax.nn.silu(raised) * backward, axis=1).astype(jnp.bfloat16)
    inner_grad = (gate_rows.astype(jnp.float32)[:, None] * backward * silu_slope(raised)).astype(jnp.bfloat16)
    contrib = lax.dot_general(inner_grad, up_matrix, (((1,), (1,)), ((), ())), preferred_element_type=jnp.float32).astype(jnp.bfloat16)
    return contrib, gate_grad


def reference(tokens, out_grad, gate_weights, expert_ids, slot_ids, up_weight, down_weight):
    entries = TOKENS * TOPK
    source = (jnp.arange(TOKENS, dtype=jnp.int32) // TOK_DEV)[:, None]
    flat_slot = ((expert_ids * DEVICES + source) * MOST + slot_ids).reshape(-1).astype(jnp.int32)
    slot_table = jnp.full((EXPERTS * DEVICES * MOST,), entries, jnp.int32)
    slot_table = slot_table.at[flat_slot].set(jnp.arange(entries, dtype=jnp.int32))
    slot_table = slot_table.reshape(EXPERTS, DEVICES * MOST)
    group_of = expert_ids // EXP_GROUP
    other_half = jnp.where(group_of == group_of[:, :1], 0, 1).astype(jnp.int32).reshape(-1)
    half_pad = jnp.concatenate([other_half, jnp.zeros((1,), jnp.int32)])
    token_pad = jnp.concatenate([tokens, jnp.zeros((1, D), jnp.bfloat16)])
    grad_pad = jnp.concatenate([out_grad, jnp.zeros((1, D), jnp.bfloat16)])
    gate_pad = jnp.concatenate([gate_weights.reshape(-1), jnp.zeros((1,), jnp.bfloat16)])

    def expert_step(carried, inputs):
        summed, gate_out = carried
        entry_row, up_matrix, down_matrix = inputs
        anchor = (entry_row // TOPK).astype(jnp.int32)
        contrib, gate_rows = expert_rows(token_pad[anchor], grad_pad[anchor], gate_pad[entry_row], up_matrix, down_matrix)
        target = jnp.where(entry_row < entries, half_pad[entry_row] * TOKENS + anchor, 2 * TOKENS).astype(jnp.int32)
        summed = summed.at[target].add(contrib.astype(jnp.float32))
        gate_out = gate_out.at[entry_row].set(gate_rows)
        return (summed, gate_out), None

    start = (jnp.zeros((2 * TOKENS + 1, D), jnp.float32), jnp.zeros((entries + 1,), jnp.bfloat16))
    (summed, gate_out), unused = lax.scan(expert_step, start, (slot_table, up_weight, down_weight))
    halves = lax.optimization_barrier(summed[:2 * TOKENS].astype(jnp.bfloat16))
    halves = halves.astype(jnp.float32).reshape(2, TOKENS, D)
    token_grad = (halves[0] + halves[1]).astype(jnp.bfloat16)
    return token_grad, gate_out[:entries].reshape(TOKENS, TOPK)
```

```python
import functools

import jax
import jax.numpy as jnp
from jax import lax
from jax.experimental import pallas as pl
from jax.experimental.pallas import tpu as pltpu
from jax.sharding import PartitionSpec as P

TOPK = 8
MESH = pl.DeviceIdType.MESH
GROUPS = 4
PEERS = 8
MIB = 1024 * 1024


def silu_slope(values):
    sigmoid_up = jax.nn.sigmoid(values)
    return sigmoid_up * (1.0 + values * (1.0 - sigmoid_up))


def expert_rows(token_rows, grad_rows, gate_rows, up_matrix, down_matrix):
    raised = jnp.dot(token_rows, up_matrix, preferred_element_type=jnp.float32)
    backward = lax.dot_general(
        grad_rows, down_matrix, (((1,), (1,)), ((), ())), preferred_element_type=jnp.float32
    )
    gate_grad = jnp.sum(jax.nn.silu(raised) * backward, axis=1).astype(jnp.bfloat16)
    inner_grad = (gate_rows.astype(jnp.float32)[:, None] * backward * silu_slope(raised)).astype(
        jnp.bfloat16
    )
    contrib = lax.dot_general(
        inner_grad, up_matrix, (((1,), (1,)), ((), ())), preferred_element_type=jnp.float32
    ).astype(jnp.bfloat16)
    return (contrib, gate_grad)


class Place:
    def __init__(self):
        self.group = lax.axis_index("group")
        self.dev = lax.axis_index("dev")
        core = self.dev % 2
        side = (self.dev // 2) % 2
        row = self.dev // 4
        self.sib = self.dev + 1 - 2 * core
        self.xn = self.dev + 2 - 4 * side
        self.yn = self.dev + 4 - 8 * row
        self.diag = self.xn + 4 - 8 * row
        self.off_sib = 1 - 2 * core

    def source(self, k):
        return lax.rem(self.group + k, GROUPS)

    def barrier(self):
        sem = pltpu.get_barrier_semaphore()
        for peer in (self.sib, self.xn, self.yn):
            pl.semaphore_signal(sem, inc=1, device_id=(self.group, peer), device_id_type=MESH)
        for k in range(1, GROUPS):
            pl.semaphore_signal(
                sem, inc=1, device_id=(self.source(k), self.dev), device_id_type=MESH
            )
        pl.semaphore_wait(sem, GROUPS + 2)


def dispatch_kernel(tok, grad, ytok, ygrad, local_sem, zs, zr, ss, rs):
    at = Place()
    at.barrier()
    pairs = ((tok, ytok), (grad, ygrad))
    g, d = at.group, at.dev

    def local(a):
        src, dst = pairs[a]
        return pltpu.make_async_copy(src.at[g], dst.at[g, d], local_sem.at[a])

    def zcopy(a, k):
        src, dst = pairs[a]
        target = lax.rem(g + GROUPS - k, GROUPS)
        return pltpu.make_async_remote_copy(
            src_ref=src.at[target], dst_ref=dst.at[g, d],
            send_sem=zs.at[a, k], recv_sem=zr.at[a, k],
            device_id=(target, d), device_id_type=MESH,
        )

    def copy(a, k, origin, slot, rel, peer):
        buf = pairs[a][1].at[at.source(k), origin]
        return pltpu.make_async_remote_copy(
            src_ref=buf, dst_ref=buf,
            send_sem=ss.at[a, k, slot], recv_sem=rs.at[a, k, rel],
            device_id=(g, peer), device_id_type=MESH,
        )

    def sends(a, k):
        first = [
            copy(a, k, d, 0, 2, at.xn),
            copy(a, k, d, 1, 4, at.yn),
            copy(a, k, d, 2, 1, at.sib),
        ]
        from_x = [copy(a, k, at.xn, 3, 3, at.sib)]
        from_y = [copy(a, k, at.yn, 4, 5, at.sib)]
        if k % 2 == 0:
            from_x.insert(0, copy(a, k, at.xn, 5, 6, at.yn))
        else:
            from_y.insert(0, copy(a, k, at.yn, 5, 6, at.xn))
        last = [copy(a, k, at.diag, 6, 7, at.sib)]
        return first, from_x, from_y, last

    def own(a, k):
        if k == 0:
            local(a).wait()
        else:
            zcopy(a, k).wait_recv()
        for c in sends(a, k)[0]:
            c.start()

    def forward(a, k):
        parts = sends(a, k)
        copy(a, k, at.xn, 0, 2, at.xn).wait_recv()
        for c in parts[1]:
            c.start()
        copy(a, k, at.yn, 1, 4, at.yn).wait_recv()
        for c in parts[2]:
            c.start()

    def forward_last(a, k):
        copy(a, k, at.diag, 5, 6, at.xn).wait_recv()
        for c in sends(a, k)[3]:
            c.start()

    order = [(0, 0), (1, 0), (0, 1), (0, 2), (0, 3), (1, 1), (1, 2), (1, 3)]
    for a in range(2):
        local(a).start()
    for k in range(1, GROUPS):
        zcopy(0, k).start()
    for i in range(len(order) + 2):
        if i < len(order):
            own(*order[i])
        if i == 1:
            for k in range(1, GROUPS):
                zcopy(1, k).start()
        if 1 <= i <= len(order):
            forward(*order[i - 1])
        if i >= 2:
            forward_last(*order[i - 2])
    for a, k in order:
        copy(a, k, at.sib, 2, 1, at.sib).wait_recv()
        copy(a, k, at.xn + at.off_sib, 3, 3, at.sib).wait_recv()
        copy(a, k, at.yn + at.off_sib, 4, 5, at.sib).wait_recv()
        copy(a, k, at.diag + at.off_sib, 6, 7, at.sib).wait_recv()
        for part in sends(a, k):
            for c in part:
                c.wait_send()
        if k:
            zcopy(a, k).wait_send()


def dispatch(tok, grad):
    groups, rows, features = tok.shape
    out = jax.ShapeDtypeStruct((groups, PEERS, rows, features), jnp.bfloat16)
    anywhere = pl.BlockSpec(memory_space=pl.ANY)
    return pl.pallas_call(
        dispatch_kernel,
        out_shape=(out, out),
        in_specs=[anywhere, anywhere],
        out_specs=(anywhere, anywhere),
        scratch_shapes=[
            pltpu.SemaphoreType.DMA((2,)),
            pltpu.SemaphoreType.DMA((2, GROUPS)),
            pltpu.SemaphoreType.DMA((2, GROUPS)),
            pltpu.SemaphoreType.DMA((2, GROUPS, 7)),
            pltpu.SemaphoreType.DMA((2, GROUPS, 8)),
        ],
        compiler_params=pltpu.CompilerParams(
            collective_id=0, has_side_effects=True, vmem_limit_bytes=4 * MIB
        ),
    )(tok, grad)


def combine_kernel(
    rows, inner, up, out, part, sib, dbuf, xbuf, ybuf, local_sem, zs, zr, ss, rs, ps, pr
):
    at = Place()
    g, d = at.group, at.dev
    features = up.shape[0]
    tile = 512
    at.barrier()

    def product(k):
        lines = inner[at.source(k)]

        @pl.loop(0, features // tile)
        def _(n):
            cols = pl.ds(pl.multiple_of(n * tile, tile), tile)
            block = lax.dot_general(
                lines, up[cols, :], (((1,), (1,)), ((), ())),
                preferred_element_type=jnp.float32,
            ).astype(jnp.bfloat16)
            part[k, :, :, cols] = block.reshape(PEERS, rows, tile)

    chips = (at.dev, at.xn, at.yn, at.diag)

    def pair(k, i):
        return pltpu.make_async_remote_copy(
            src_ref=part.at[k, chips[i] + at.off_sib], dst_ref=sib.at[k, i],
            send_sem=ps.at[k, i], recv_sem=pr.at[k, i],
            device_id=(g, at.sib), device_id_type=MESH,
        )

    def to(k, slot, origin, buf, peer):
        return pltpu.make_async_remote_copy(
            src_ref=part.at[k, origin], dst_ref=buf.at[k],
            send_sem=ss.at[k, slot], recv_sem=rs.at[k, slot],
            device_id=(g, peer), device_id_type=MESH,
        )

    def to_x(k):
        return to(k, 0, at.xn, xbuf, at.xn)

    def to_y(k):
        return to(k, 1, at.yn, ybuf, at.yn)

    def to_far(k):
        return to(k, 2, at.diag, dbuf, at.xn if k % 2 == 0 else at.yn)

    def add(k, origin, *terms):
        @pl.loop(0, rows // 16)
        def _(r):
            lines = pl.ds(pl.multiple_of(r * 16, 16), 16)
            total = part[k, origin, lines, :].astype(jnp.float32)
            for buf, index in terms:
                total = total + buf[index + (lines,)].astype(jnp.float32)
            part[k, origin, lines, :] = total.astype(jnp.bfloat16)

    def start_pairs(k):
        for i in (3, 1, 2, 0):
            pair(k, i).start()

    def first(k):
        for i in (3, 1, 2, 0):
            pair(k, i).wait_recv()
            if i == 3:
                add(k, at.diag, (sib, (k, 3)))
                to_far(k).start()
            elif i == 1:
                add(k, at.xn, (sib, (k, 1)))
                if k % 2 == 0:
                    to_x(k).start()
            elif i == 2:
                add(k, at.yn, (sib, (k, 2)))
                if k % 2 == 1:
                    to_y(k).start()

    def second(k):
        to_far(k).wait_recv()
        if k % 2 == 0:
            add(k, at.yn, (dbuf, (k,)))
            to_y(k).start()
        else:
            add(k, at.xn, (dbuf, (k,)))
            to_x(k).start()

    def home(k):
        target = at.source(k)
        return pltpu.make_async_remote_copy(
            src_ref=part.at[k, d], dst_ref=out.at[g],
            send_sem=zs.at[k], recv_sem=zr.at[k],
            device_id=(target, d), device_id_type=MESH,
        )

    def local():
        return pltpu.make_async_copy(part.at[0, d], out.at[g], local_sem)

    def third(k):
        to_x(k).wait_recv()
        to_y(k).wait_recv()
        add(k, d, (sib, (k, 0)), (xbuf, (k,)), (ybuf, (k,)))
        if k:
            home(k).start()
        else:
            local().start()

    order = (2, 1, 3, 0)
    for i in range(len(order) + 3):
        if i < len(order):
            product(order[i])
            start_pairs(order[i])
        if 1 <= i <= len(order):
            first(order[i - 1])
        if 2 <= i <= len(order) + 1:
            second(order[i - 2])
        if i >= 3:
            third(order[i - 3])
    for k in order:
        for i in range(4):
            pair(k, i).wait_send()
        to_x(k).wait_send()
        to_y(k).wait_send()
        to_far(k).wait_send()
        if k:
            home(k).wait_send()
            home(k).wait_recv()
    local().wait()


def combine(inner, up_matrix, rows):
    features = up_matrix.shape[0]
    whole = pl.BlockSpec(memory_space=pltpu.VMEM)
    hop = pltpu.VMEM((GROUPS, rows, features), jnp.bfloat16)
    return pl.pallas_call(
        functools.partial(combine_kernel, rows),
        out_shape=jax.ShapeDtypeStruct((GROUPS, rows, features), jnp.bfloat16),
        in_specs=[whole, whole],
        out_specs=pl.BlockSpec(memory_space=pl.ANY),
        scratch_shapes=[
            pltpu.VMEM((GROUPS, PEERS, rows, features), jnp.bfloat16),
            pltpu.VMEM((GROUPS, 4, rows, features), jnp.bfloat16),
            hop,
            hop,
            hop,
            pltpu.SemaphoreType.DMA,
            pltpu.SemaphoreType.DMA((GROUPS,)),
            pltpu.SemaphoreType.DMA((GROUPS,)),
            pltpu.SemaphoreType.DMA((GROUPS, 3)),
            pltpu.SemaphoreType.DMA((GROUPS, 3)),
            pltpu.SemaphoreType.DMA((GROUPS, 4)),
            pltpu.SemaphoreType.DMA((GROUPS, 4)),
        ],
        compiler_params=pltpu.CompilerParams(
            collective_id=1, has_side_effects=True, vmem_limit_bytes=58 * MIB
        ),
    )(inner, up_matrix)


def grouped(tokens, out_grad, gate_weights, expert_ids, slot_ids, up_weight, down_weight):
    rows_dev, features = tokens.shape
    hidden = up_weight.shape[2]
    experts = GROUPS * PEERS
    rows = 5 * rows_dev // 8
    up_matrix = up_weight[0]
    down_matrix = down_weight[0]
    names = expert_ids[:, :, None] == jnp.arange(experts, dtype=jnp.int32)
    in_group = jnp.any(
        (expert_ids // PEERS)[:, :, None] == jnp.arange(GROUPS, dtype=jnp.int32), axis=1
    )
    before = jnp.arange(rows_dev)[:, None] > jnp.arange(rows_dev)[None, :]
    rank = jnp.dot(
        before.astype(jnp.bfloat16), in_group.astype(jnp.bfloat16),
        preferred_element_type=jnp.float32,
    ).astype(jnp.int32)
    pick = jnp.logical_and(
        in_group[:, :, None],
        rank[:, :, None] == jnp.arange(rows, dtype=jnp.int32),
    ).astype(jnp.bfloat16)

    def packed(values):
        return jnp.einsum(
            "tgp,td->gpd", pick, values, preferred_element_type=jnp.float32
        ).astype(jnp.bfloat16)

    gate_table = jnp.sum(
        jnp.where(names, gate_weights.astype(jnp.float32)[:, :, None], 0.0), axis=1
    ).astype(jnp.bfloat16)
    gate_send = jnp.einsum(
        "tgp,tge->gep", pick, gate_table.reshape(rows_dev, GROUPS, PEERS),
        preferred_element_type=jnp.float32,
    ).astype(jnp.bfloat16)
    gate_rows = lax.all_to_all(
        gate_send.reshape(experts, rows), ("group", "dev"), 0, 0, tiled=True
    ).reshape(-1)
    token_rows, grad_rows = dispatch(packed(tokens), packed(out_grad))
    raised = jnp.dot(
        token_rows.reshape(-1, features), up_matrix, preferred_element_type=jnp.float32
    )
    backward = lax.dot_general(
        grad_rows.reshape(-1, features), down_matrix, (((1,), (1,)), ((), ())),
        preferred_element_type=jnp.float32,
    )
    gate_out = jnp.sum(jax.nn.silu(raised) * backward, axis=1).astype(jnp.bfloat16)
    inner = (gate_rows.astype(jnp.float32)[:, None] * backward * silu_slope(raised)).astype(
        jnp.bfloat16
    )
    gate_back = lax.all_to_all(
        gate_out.reshape(experts, rows), ("group", "dev"), 0, 0, tiled=True
    )
    halves = combine(inner.reshape(GROUPS, PEERS * rows, hidden), up_matrix, rows)
    gate_tokens = jnp.einsum(
        "tgp,gep->tge", pick, gate_back.reshape(GROUPS, PEERS, rows),
        preferred_element_type=jnp.float32,
    ).reshape(rows_dev, experts)
    gate_grad = jnp.sum(jnp.where(names, gate_tokens[:, None, :], 0.0), axis=2).astype(
        jnp.bfloat16
    )
    token_grad = jnp.einsum(
        "tgp,gpd->td", pick, halves, preferred_element_type=jnp.float32
    ).astype(jnp.bfloat16)
    return (token_grad, gate_grad)


def shards(tokens, out_grad, gate_weights, expert_ids, slot_ids, up_weight, down_weight):
    rows_dev = tokens.shape[0]
    features = tokens.shape[1]
    groups = lax.axis_size("group")
    per_group = lax.axis_size("dev")
    experts = groups * per_group
    capacity = 5 * rows_dev * TOPK // (4 * experts)
    slots_all = experts * capacity
    entries = rows_dev * TOPK
    up_matrix = up_weight[0]
    down_matrix = down_weight[0]
    group_of = expert_ids // per_group
    zero_row = jnp.zeros((1, features), jnp.bfloat16)
    token_pad = jnp.concatenate([tokens, zero_row])
    grad_pad = jnp.concatenate([out_grad, zero_row])
    gate_flat = jnp.concatenate([gate_weights.reshape(-1), jnp.zeros((1,), jnp.bfloat16)])
    target = (expert_ids * capacity + slot_ids).reshape(-1)
    slot_table = (
        jnp.full((slots_all,), entries, jnp.int32)
        .at[target]
        .set(jnp.arange(entries, dtype=jnp.int32))
    )
    anchor = slot_table // TOPK
    arrived = (
        lax.all_to_all(
            token_pad[anchor].reshape(experts, capacity, features),
            ("group", "dev"),
            split_axis=0,
            concat_axis=0,
            tiled=True,
        ),
        lax.all_to_all(
            grad_pad[anchor].reshape(experts, capacity, features),
            ("group", "dev"),
            split_axis=0,
            concat_axis=0,
            tiled=True,
        ),
        lax.all_to_all(
            gate_flat[slot_table].reshape(experts, capacity),
            ("group", "dev"),
            split_axis=0,
            concat_axis=0,
            tiled=True,
        ),
    )
    contrib, gate_rows = expert_rows(
        arrived[0].reshape(slots_all, features),
        arrived[1].reshape(slots_all, features),
        arrived[2].reshape(slots_all),
        up_matrix,
        down_matrix,
    )
    returned_rows = (
        lax.all_to_all(
            contrib.reshape(experts, capacity, features),
            ("group", "dev"),
            split_axis=0,
            concat_axis=0,
            tiled=True,
        ),
        lax.all_to_all(
            gate_rows.reshape(experts, capacity),
            ("group", "dev"),
            split_axis=0,
            concat_axis=0,
            tiled=True,
        ),
    )
    gathered = (
        returned_rows[0].reshape(slots_all, features)[target].reshape(rows_dev, TOPK, features)
    )
    gate_grad = returned_rows[1].reshape(-1)[target].reshape(rows_dev, TOPK)
    same_group = group_of == group_of[:, :1]
    selector = jnp.stack([same_group, jnp.logical_not(same_group)], axis=1).astype(jnp.bfloat16)
    halves = jnp.einsum(
        "tpk,tkd->tpd", selector, gathered, preferred_element_type=jnp.float32
    ).astype(jnp.bfloat16)
    token_grad = jnp.sum(halves.astype(jnp.float32), axis=1).astype(jnp.bfloat16)
    return (token_grad, gate_grad)


def solution(mesh):
    in_specs = (
        P(("group", "dev"), None),
        P(("group", "dev"), None),
        P(("group", "dev"), None),
        P(("group", "dev"), None),
        P(("group", "dev"), None),
        P(("group", "dev"), None, None),
        P(("group", "dev"), None, None),
    )
    out_specs = (P(("group", "dev"), None), P(("group", "dev"), None))
    fits = mesh.shape["group"] == GROUPS and mesh.shape["dev"] == PEERS
    step = grouped if fits else shards
    return jax.shard_map(step, mesh=mesh, in_specs=in_specs, out_specs=out_specs, check_vma=False)
```

```python
import functools

import jax
import jax.numpy as jnp
from jax import lax
from jax.experimental import pallas as pl
from jax.experimental.pallas import tpu as pltpu
from jax.sharding import PartitionSpec as P

TOPK = 8
MESH = pl.DeviceIdType.MESH
GROUPS = 4
PEERS = 8
LANES = 128
MIB = 1024 * 1024


def silu_slope(values):
    sigmoid_up = jax.nn.sigmoid(values)
    return sigmoid_up * (1.0 + values * (1.0 - sigmoid_up))


def expert_rows(token_rows, grad_rows, gate_rows, up_matrix, down_matrix):
    raised = jnp.dot(token_rows, up_matrix, preferred_element_type=jnp.float32)
    backward = lax.dot_general(
        grad_rows, down_matrix, (((1,), (1,)), ((), ())), preferred_element_type=jnp.float32
    )
    gate_grad = jnp.sum(jax.nn.silu(raised) * backward, axis=1).astype(jnp.bfloat16)
    inner_grad = (gate_rows.astype(jnp.float32)[:, None] * backward * silu_slope(raised)).astype(
        jnp.bfloat16
    )
    contrib = lax.dot_general(
        inner_grad, up_matrix, (((1,), (1,)), ((), ())), preferred_element_type=jnp.float32
    ).astype(jnp.bfloat16)
    return (contrib, gate_grad)


class Place:
    def __init__(self):
        self.group = lax.axis_index("group")
        self.dev = lax.axis_index("dev")
        core = self.dev % 2
        side = (self.dev // 2) % 2
        row = self.dev // 4
        self.sib = self.dev + 1 - 2 * core
        self.xn = self.dev + 2 - 4 * side
        self.yn = self.dev + 4 - 8 * row
        self.diag = self.xn + 4 - 8 * row
        self.off_sib = 1 - 2 * core

    def source(self, k):
        return lax.rem(self.group + k, GROUPS)

    def barrier(self):
        sem = pltpu.get_barrier_semaphore()
        for peer in (self.sib, self.xn, self.yn):
            pl.semaphore_signal(sem, inc=1, device_id=(self.group, peer), device_id_type=MESH)
        for k in range(1, GROUPS):
            pl.semaphore_signal(
                sem, inc=1, device_id=(self.source(k), self.dev), device_id_type=MESH
            )
        pl.semaphore_wait(sem, GROUPS + 2)


def dispatch_kernel(
    rows, tok, grad, up_hbm, down_hbm, ytok, ygrad, inner, gate_out,
    up, down, tok_buf, grad_buf, raised, gate, total,
    local_sem, weight_sem, load_sem, zs, zr, ss, rs,
):
    at = Place()
    g, d = at.group, at.dev
    tile = 256
    features, hidden = up.shape
    up_load = pltpu.make_async_copy(up_hbm, up, weight_sem.at[0])
    down_load = pltpu.make_async_copy(down_hbm, down, weight_sem.at[1])
    at.barrier()
    pairs = ((tok, ytok), (grad, ygrad))

    def lines_of(origin):
        return pl.ds(pl.multiple_of(origin * rows, 16), rows)

    def local(a):
        src, dst = pairs[a]
        return pltpu.make_async_copy(src.at[g], dst.at[g, lines_of(d)], local_sem.at[a])

    def zcopy(a, k):
        src, dst = pairs[a]
        target = lax.rem(g + GROUPS - k, GROUPS)
        return pltpu.make_async_remote_copy(
            src_ref=src.at[target], dst_ref=dst.at[g, lines_of(d)],
            send_sem=zs.at[a, k], recv_sem=zr.at[a, k],
            device_id=(target, d), device_id_type=MESH,
        )

    def copy(a, k, origin, slot, rel, peer):
        buf = pairs[a][1].at[at.source(k), lines_of(origin)]
        return pltpu.make_async_remote_copy(
            src_ref=buf, dst_ref=buf,
            send_sem=ss.at[a, k, slot], recv_sem=rs.at[a, k, rel],
            device_id=(g, peer), device_id_type=MESH,
        )

    def far(a, k):
        if k % 2 == 0:
            return copy(a, k, at.xn, 5, 6, at.yn)
        return copy(a, k, at.yn, 5, 6, at.xn)

    def own(a, k):
        if k == 0:
            local(a).wait()
        else:
            zcopy(a, k).wait_recv()
        copy(a, k, d, 0, 2, at.xn).start()
        copy(a, k, d, 1, 4, at.yn).start()
        copy(a, k, d, 2, 1, at.sib).start()

    def forward(a, k):
        copy(a, k, at.xn, 0, 2, at.xn).wait_recv()
        if k % 2 == 0:
            far(a, k).start()
        copy(a, k, at.xn, 3, 3, at.sib).start()
        copy(a, k, at.yn, 1, 4, at.yn).wait_recv()
        if k % 2 == 1:
            far(a, k).start()
        copy(a, k, at.yn, 4, 5, at.sib).start()

    def forward_last(a, k):
        copy(a, k, at.diag, 5, 6, at.xn).wait_recv()
        copy(a, k, at.diag, 6, 7, at.sib).start()

    def load(a, k):
        buf = tok_buf if a == 0 else grad_buf
        return pltpu.make_async_copy(pairs[a][1].at[at.source(k)], buf, load_sem.at[a])

    def finish(a, k):
        copy(a, k, at.sib, 2, 1, at.sib).wait_recv()
        copy(a, k, at.xn + at.off_sib, 3, 3, at.sib).wait_recv()
        copy(a, k, at.yn + at.off_sib, 4, 5, at.sib).wait_recv()
        copy(a, k, at.diag + at.off_sib, 6, 7, at.sib).wait_recv()
        load(a, k).start()

    def raise_rows(k):
        mine = lax.broadcasted_iota(jnp.int32, gate.shape[1:], 1) == d
        held = jnp.where(mine, tok_buf[:, features:].astype(jnp.float32), 0.0)
        gate[k] = jnp.broadcast_to(jnp.sum(held, axis=1, keepdims=True), gate.shape[1:])

        @pl.loop(0, hidden // tile)
        def _(n):
            cols = pl.ds(pl.multiple_of(n * tile, tile), tile)
            raised[k, :, cols] = jnp.dot(
                tok_buf[:, :features], up[:, cols], preferred_element_type=jnp.float32
            )

    def lower_rows(k):
        total[...] = jnp.zeros_like(total)

        @pl.loop(0, hidden // tile)
        def _(n):
            cols = pl.ds(pl.multiple_of(n * tile, tile), tile)
            backward = lax.dot_general(
                grad_buf[...], down[cols, :], (((1,), (1,)), ((), ())),
                preferred_element_type=jnp.float32,
            )
            value = raised[k, :, cols]
            sig = jax.nn.sigmoid(value)
            terms = value * sig * backward
            total[...] += terms[:, :128] + terms[:, 128:]
            slope = sig * (1.0 + value * (1.0 - sig))
            inner[at.source(k), :, cols] = (gate[k][:, :1] * backward * slope).astype(
                jnp.bfloat16
            )

        mine = lax.broadcasted_iota(jnp.int32, total.shape, 1) == d
        summed = jnp.sum(total[...], axis=1, keepdims=True)
        gate_out[at.source(k)] = jnp.where(mine, summed, 0.0).astype(jnp.bfloat16)

    def compute(a, k):
        load(a, k).wait()
        if (a, k) == order[0]:
            up_load.wait()
        if (a, k) == order[1]:
            down_load.wait()
        if a == 0:
            raise_rows(k)
        else:
            lower_rows(k)

    order = [(0, 0), (1, 0), (0, 1), (0, 2), (0, 3), (1, 1), (1, 2), (1, 3)]
    steps = len(order)
    for a in range(2):
        local(a).start()
    for k in range(1, GROUPS):
        zcopy(0, k).start()
    for i in range(steps + 4):
        if i < steps:
            own(*order[i])
        if i == 1:
            for k in range(1, GROUPS):
                zcopy(1, k).start()
            up_load.start()
            down_load.start()
        if 1 <= i <= steps:
            forward(*order[i - 1])
        if 2 <= i <= steps + 1:
            forward_last(*order[i - 2])
        if i >= 4:
            compute(*order[i - 4])
        if 3 <= i <= steps + 2:
            finish(*order[i - 3])
    for a, k in order:
        copy(a, k, d, 0, 2, at.xn).wait_send()
        copy(a, k, d, 1, 4, at.yn).wait_send()
        copy(a, k, d, 2, 1, at.sib).wait_send()
        copy(a, k, at.xn, 3, 3, at.sib).wait_send()
        copy(a, k, at.yn, 4, 5, at.sib).wait_send()
        far(a, k).wait_send()
        copy(a, k, at.diag, 6, 7, at.sib).wait_send()
        if k:
            zcopy(a, k).wait_send()


def dispatch(tok, grad, up_matrix, down_matrix):
    groups, rows, wide = tok.shape
    features, hidden = up_matrix.shape
    lines = PEERS * rows
    anywhere = pl.BlockSpec(memory_space=pl.ANY)
    whole = pl.BlockSpec(memory_space=pltpu.VMEM)
    return pl.pallas_call(
        functools.partial(dispatch_kernel, rows),
        out_shape=(
            jax.ShapeDtypeStruct((groups, lines, wide), jnp.bfloat16),
            jax.ShapeDtypeStruct((groups, lines, features), jnp.bfloat16),
            jax.ShapeDtypeStruct((groups, lines, hidden), jnp.bfloat16),
            jax.ShapeDtypeStruct((groups, lines, LANES), jnp.bfloat16),
        ),
        in_specs=[anywhere] * 4,
        out_specs=(anywhere, anywhere, whole, whole),
        scratch_shapes=[
            pltpu.VMEM((features, hidden), jnp.bfloat16),
            pltpu.VMEM((hidden, features), jnp.bfloat16),
            pltpu.VMEM((lines, wide), jnp.bfloat16),
            pltpu.VMEM((lines, features), jnp.bfloat16),
            pltpu.VMEM((groups, lines, hidden), jnp.float32),
            pltpu.VMEM((groups, lines, LANES), jnp.float32),
            pltpu.VMEM((lines, LANES), jnp.float32),
            pltpu.SemaphoreType.DMA((2,)),
            pltpu.SemaphoreType.DMA((2,)),
            pltpu.SemaphoreType.DMA((2,)),
            pltpu.SemaphoreType.DMA((2, GROUPS)),
            pltpu.SemaphoreType.DMA((2, GROUPS)),
            pltpu.SemaphoreType.DMA((2, GROUPS, 7)),
            pltpu.SemaphoreType.DMA((2, GROUPS, 8)),
        ],
        compiler_params=pltpu.CompilerParams(
            collective_id=0, has_side_effects=True, vmem_limit_bytes=58 * MIB
        ),
    )(tok, grad, up_matrix, down_matrix)


def combine_kernel(
    rows, inner, gates, up, out, part, sib, dbuf, xbuf, ybuf, local_sem, zs, zr, ss, rs, ps, pr
):
    at = Place()
    g, d = at.group, at.dev
    features = up.shape[0]
    tile = 512
    at.barrier()

    def product(k):
        lines = inner[at.source(k)]

        @pl.loop(0, features // tile)
        def _(n):
            cols = pl.ds(pl.multiple_of(n * tile, tile), tile)
            block = lax.dot_general(
                lines, up[cols, :], (((1,), (1,)), ((), ())),
                preferred_element_type=jnp.float32,
            ).astype(jnp.bfloat16)
            part[k, :, :, cols] = block.reshape(PEERS, rows, tile)

        part[k, :, :, features:] = gates[at.source(k)].reshape(PEERS, rows, LANES)

    chips = (at.dev, at.xn, at.yn, at.diag)

    def pair(k, i):
        return pltpu.make_async_remote_copy(
            src_ref=part.at[k, chips[i] + at.off_sib], dst_ref=sib.at[k, i],
            send_sem=ps.at[k, i], recv_sem=pr.at[k, i],
            device_id=(g, at.sib), device_id_type=MESH,
        )

    def to(k, slot, origin, buf, peer):
        return pltpu.make_async_remote_copy(
            src_ref=part.at[k, origin], dst_ref=buf.at[k],
            send_sem=ss.at[k, slot], recv_sem=rs.at[k, slot],
            device_id=(g, peer), device_id_type=MESH,
        )

    def to_x(k):
        return to(k, 0, at.xn, xbuf, at.xn)

    def to_y(k):
        return to(k, 1, at.yn, ybuf, at.yn)

    def to_far(k):
        return to(k, 2, at.diag, dbuf, at.xn if k % 2 == 0 else at.yn)

    def add(k, origin, *terms):
        @pl.loop(0, rows // 16)
        def _(r):
            lines = pl.ds(pl.multiple_of(r * 16, 16), 16)
            total = part[k, origin, lines, :].astype(jnp.float32)
            for buf, index in terms:
                total = total + buf[index + (lines,)].astype(jnp.float32)
            part[k, origin, lines, :] = total.astype(jnp.bfloat16)

    def start_pairs(k):
        for i in (3, 1, 2, 0):
            pair(k, i).start()

    def first(k):
        for i in (3, 1, 2, 0):
            pair(k, i).wait_recv()
            if i == 3:
                add(k, at.diag, (sib, (k, 3)))
                to_far(k).start()
            elif i == 1:
                add(k, at.xn, (sib, (k, 1)))
                if k % 2 == 0:
                    to_x(k).start()
            elif i == 2:
                add(k, at.yn, (sib, (k, 2)))
                if k % 2 == 1:
                    to_y(k).start()

    def second(k):
        to_far(k).wait_recv()
        if k % 2 == 0:
            add(k, at.yn, (dbuf, (k,)))
            to_y(k).start()
        else:
            add(k, at.xn, (dbuf, (k,)))
            to_x(k).start()

    def home(k):
        target = at.source(k)
        return pltpu.make_async_remote_copy(
            src_ref=part.at[k, d], dst_ref=out.at[g],
            send_sem=zs.at[k], recv_sem=zr.at[k],
            device_id=(target, d), device_id_type=MESH,
        )

    def local():
        return pltpu.make_async_copy(part.at[0, d], out.at[g], local_sem)

    def third(k):
        to_x(k).wait_recv()
        to_y(k).wait_recv()
        add(k, d, (sib, (k, 0)), (xbuf, (k,)), (ybuf, (k,)))
        if k:
            home(k).start()
        else:
            local().start()

    order = (2, 1, 3, 0)
    for i in range(len(order) + 3):
        if i < len(order):
            product(order[i])
            start_pairs(order[i])
        if 1 <= i <= len(order):
            first(order[i - 1])
        if 2 <= i <= len(order) + 1:
            second(order[i - 2])
        if i >= 3:
            third(order[i - 3])
    for k in order:
        for i in range(4):
            pair(k, i).wait_send()
        to_x(k).wait_send()
        to_y(k).wait_send()
        to_far(k).wait_send()
        if k:
            home(k).wait_send()
            home(k).wait_recv()
    local().wait()


def combine(inner, gates, up_matrix, rows):
    wide = up_matrix.shape[0] + LANES
    whole = pl.BlockSpec(memory_space=pltpu.VMEM)
    hop = pltpu.VMEM((GROUPS, rows, wide), jnp.bfloat16)
    return pl.pallas_call(
        functools.partial(combine_kernel, rows),
        out_shape=jax.ShapeDtypeStruct((GROUPS, rows, wide), jnp.bfloat16),
        in_specs=[whole, whole, whole],
        out_specs=pl.BlockSpec(memory_space=pl.ANY),
        scratch_shapes=[
            pltpu.VMEM((GROUPS, PEERS, rows, wide), jnp.bfloat16),
            pltpu.VMEM((GROUPS, 4, rows, wide), jnp.bfloat16),
            hop,
            hop,
            hop,
            pltpu.SemaphoreType.DMA,
            pltpu.SemaphoreType.DMA((GROUPS,)),
            pltpu.SemaphoreType.DMA((GROUPS,)),
            pltpu.SemaphoreType.DMA((GROUPS, 3)),
            pltpu.SemaphoreType.DMA((GROUPS, 3)),
            pltpu.SemaphoreType.DMA((GROUPS, 4)),
            pltpu.SemaphoreType.DMA((GROUPS, 4)),
        ],
        compiler_params=pltpu.CompilerParams(
            collective_id=1, has_side_effects=True, vmem_limit_bytes=58 * MIB
        ),
    )(inner, gates, up_matrix)


def grouped(tokens, out_grad, gate_weights, expert_ids, slot_ids, up_weight, down_weight):
    rows_dev, features = tokens.shape
    experts = GROUPS * PEERS
    rows = 5 * rows_dev // 8
    up_matrix = up_weight[0]
    down_matrix = down_weight[0]
    names = expert_ids[:, :, None] == jnp.arange(experts, dtype=jnp.int32)
    in_group = jnp.any(
        (expert_ids // PEERS)[:, :, None] == jnp.arange(GROUPS, dtype=jnp.int32), axis=1
    )
    before = jnp.arange(rows_dev)[:, None] > jnp.arange(rows_dev)[None, :]
    rank = jnp.dot(
        before.astype(jnp.bfloat16), in_group.astype(jnp.bfloat16),
        preferred_element_type=jnp.float32,
    ).astype(jnp.int32)
    pick = jnp.logical_and(
        in_group[:, :, None],
        rank[:, :, None] == jnp.arange(rows, dtype=jnp.int32),
    ).astype(jnp.bfloat16)

    def packed(values):
        return jnp.einsum(
            "tgp,td->gpd", pick, values, preferred_element_type=jnp.float32
        ).astype(jnp.bfloat16)

    gate_table = jnp.sum(
        jnp.where(names, gate_weights.astype(jnp.float32)[:, :, None], 0.0), axis=1
    ).astype(jnp.bfloat16)
    gate_lanes = jnp.pad(
        gate_table.reshape(rows_dev, GROUPS, PEERS), ((0, 0), (0, 0), (0, LANES - PEERS))
    )
    gate_send = jnp.einsum(
        "tgp,tge->gpe", pick, gate_lanes, preferred_element_type=jnp.float32
    ).astype(jnp.bfloat16)
    inner, gates = dispatch(
        jnp.concatenate([packed(tokens), gate_send], axis=2),
        packed(out_grad),
        up_matrix,
        down_matrix,
    )[2:]
    halves = combine(inner, gates, up_matrix, rows)
    gate_tokens = jnp.einsum(
        "tgp,gpe->tge", pick, halves[:, :, features : features + PEERS],
        preferred_element_type=jnp.float32,
    ).reshape(rows_dev, experts)
    gate_grad = jnp.sum(jnp.where(names, gate_tokens[:, None, :], 0.0), axis=2).astype(
        jnp.bfloat16
    )
    token_grad = jnp.einsum(
        "tgp,gpd->td", pick, halves[:, :, :features], preferred_element_type=jnp.float32
    ).astype(jnp.bfloat16)
    return (token_grad, gate_grad)


def shards(tokens, out_grad, gate_weights, expert_ids, slot_ids, up_weight, down_weight):
    rows_dev = tokens.shape[0]
    features = tokens.shape[1]
    groups = lax.axis_size("group")
    per_group = lax.axis_size("dev")
    experts = groups * per_group
    capacity = 5 * rows_dev * TOPK // (4 * experts)
    slots_all = experts * capacity
    entries = rows_dev * TOPK
    up_matrix = up_weight[0]
    down_matrix = down_weight[0]
    group_of = expert_ids // per_group
    zero_row = jnp.zeros((1, features), jnp.bfloat16)
    token_pad = jnp.concatenate([tokens, zero_row])
    grad_pad = jnp.concatenate([out_grad, zero_row])
    gate_flat = jnp.concatenate([gate_weights.reshape(-1), jnp.zeros((1,), jnp.bfloat16)])
    target = (expert_ids * capacity + slot_ids).reshape(-1)
    slot_table = (
        jnp.full((slots_all,), entries, jnp.int32)
        .at[target]
        .set(jnp.arange(entries, dtype=jnp.int32))
    )
    anchor = slot_table // TOPK
    arrived = (
        lax.all_to_all(
            token_pad[anchor].reshape(experts, capacity, features),
            ("group", "dev"),
            split_axis=0,
            concat_axis=0,
            tiled=True,
        ),
        lax.all_to_all(
            grad_pad[anchor].reshape(experts, capacity, features),
            ("group", "dev"),
            split_axis=0,
            concat_axis=0,
            tiled=True,
        ),
        lax.all_to_all(
            gate_flat[slot_table].reshape(experts, capacity),
            ("group", "dev"),
            split_axis=0,
            concat_axis=0,
            tiled=True,
        ),
    )
    contrib, gate_rows = expert_rows(
        arrived[0].reshape(slots_all, features),
        arrived[1].reshape(slots_all, features),
        arrived[2].reshape(slots_all),
        up_matrix,
        down_matrix,
    )
    returned_rows = (
        lax.all_to_all(
            contrib.reshape(experts, capacity, features),
            ("group", "dev"),
            split_axis=0,
            concat_axis=0,
            tiled=True,
        ),
        lax.all_to_all(
            gate_rows.reshape(experts, capacity),
            ("group", "dev"),
            split_axis=0,
            concat_axis=0,
            tiled=True,
        ),
    )
    gathered = (
        returned_rows[0].reshape(slots_all, features)[target].reshape(rows_dev, TOPK, features)
    )
    gate_grad = returned_rows[1].reshape(-1)[target].reshape(rows_dev, TOPK)
    same_group = group_of == group_of[:, :1]
    selector = jnp.stack([same_group, jnp.logical_not(same_group)], axis=1).astype(jnp.bfloat16)
    halves = jnp.einsum(
        "tpk,tkd->tpd", selector, gathered, preferred_element_type=jnp.float32
    ).astype(jnp.bfloat16)
    token_grad = jnp.sum(halves.astype(jnp.float32), axis=1).astype(jnp.bfloat16)
    return (token_grad, gate_grad)


def solution(mesh):
    in_specs = (
        P(("group", "dev"), None),
        P(("group", "dev"), None),
        P(("group", "dev"), None),
        P(("group", "dev"), None),
        P(("group", "dev"), None),
        P(("group", "dev"), None, None),
        P(("group", "dev"), None, None),
    )
    out_specs = (P(("group", "dev"), None), P(("group", "dev"), None))
    fits = mesh.shape["group"] == GROUPS and mesh.shape["dev"] == PEERS
    step = grouped if fits else shards
    return jax.shard_map(step, mesh=mesh, in_specs=in_specs, out_specs=out_specs, check_vma=False)
```

```python
import functools

import jax
import jax.numpy as jnp
from jax import lax
from jax.experimental import pallas as pl
from jax.experimental.pallas import tpu as pltpu
from jax.sharding import PartitionSpec as P

TOPK = 8
MESH = pl.DeviceIdType.MESH
GROUPS = 4
PEERS = 8
LANES = 128
MIB = 1024 * 1024


def silu_slope(values):
    sigmoid_up = jax.nn.sigmoid(values)
    return sigmoid_up * (1.0 + values * (1.0 - sigmoid_up))


def expert_rows(token_rows, grad_rows, gate_rows, up_matrix, down_matrix):
    raised = jnp.dot(token_rows, up_matrix, preferred_element_type=jnp.float32)
    backward = lax.dot_general(
        grad_rows, down_matrix, (((1,), (1,)), ((), ())), preferred_element_type=jnp.float32
    )
    gate_grad = jnp.sum(jax.nn.silu(raised) * backward, axis=1).astype(jnp.bfloat16)
    inner_grad = (gate_rows.astype(jnp.float32)[:, None] * backward * silu_slope(raised)).astype(
        jnp.bfloat16
    )
    contrib = lax.dot_general(
        inner_grad, up_matrix, (((1,), (1,)), ((), ())), preferred_element_type=jnp.float32
    ).astype(jnp.bfloat16)
    return (contrib, gate_grad)


class Place:
    def __init__(self):
        self.group = lax.axis_index("group")
        self.dev = lax.axis_index("dev")
        core = self.dev % 2
        side = (self.dev // 2) % 2
        row = self.dev // 4
        self.sib = self.dev + 1 - 2 * core
        self.xn = self.dev + 2 - 4 * side
        self.yn = self.dev + 4 - 8 * row
        self.diag = self.xn + 4 - 8 * row
        self.off_sib = 1 - 2 * core

    def source(self, k):
        return lax.rem(self.group + k, GROUPS)

    def barrier(self):
        sem = pltpu.get_barrier_semaphore()
        for peer in (self.sib, self.xn, self.yn):
            pl.semaphore_signal(sem, inc=1, device_id=(self.group, peer), device_id_type=MESH)
        for k in range(1, GROUPS):
            pl.semaphore_signal(
                sem, inc=1, device_id=(self.source(k), self.dev), device_id_type=MESH
            )
        pl.semaphore_wait(sem, GROUPS + 2)


def dispatch_kernel(
    rows, tok, grad, up_hbm, down_hbm, ytok, ygrad, inner, gate_out,
    up, down, tok_buf, grad_buf, raised, gate, total,
    local_sem, weight_sem, load_sem, zs, zr, ss, rs,
):
    at = Place()
    g, d = at.group, at.dev
    tile = 256
    features, hidden = up.shape
    up_load = pltpu.make_async_copy(up_hbm, up, weight_sem.at[0])
    down_load = pltpu.make_async_copy(down_hbm, down, weight_sem.at[1])
    at.barrier()
    pairs = ((tok, ytok), (grad, ygrad))

    def lines_of(origin):
        return pl.ds(pl.multiple_of(origin * rows, 16), rows)

    def local(a):
        src, dst = pairs[a]
        return pltpu.make_async_copy(src.at[g], dst.at[g, lines_of(d)], local_sem.at[a])

    def zcopy(a, k):
        src, dst = pairs[a]
        target = lax.rem(g + GROUPS - k, GROUPS)
        return pltpu.make_async_remote_copy(
            src_ref=src.at[target], dst_ref=dst.at[g, lines_of(d)],
            send_sem=zs.at[a, k], recv_sem=zr.at[a, k],
            device_id=(target, d), device_id_type=MESH,
        )

    def copy(a, k, origin, slot, rel, peer):
        buf = pairs[a][1].at[at.source(k), lines_of(origin)]
        return pltpu.make_async_remote_copy(
            src_ref=buf, dst_ref=buf,
            send_sem=ss.at[a, k, slot], recv_sem=rs.at[a, k, rel],
            device_id=(g, peer), device_id_type=MESH,
        )

    def far(a, k):
        if k % 2 == 0:
            return copy(a, k, at.xn, 5, 6, at.yn)
        return copy(a, k, at.yn, 5, 6, at.xn)

    def own(a, k):
        if k == 0:
            local(a).wait()
        else:
            zcopy(a, k).wait_recv()
        copy(a, k, d, 0, 2, at.xn).start()
        copy(a, k, d, 1, 4, at.yn).start()
        copy(a, k, d, 2, 1, at.sib).start()

    def forward(a, k):
        copy(a, k, at.xn, 0, 2, at.xn).wait_recv()
        if k % 2 == 0:
            far(a, k).start()
        copy(a, k, at.xn, 3, 3, at.sib).start()
        copy(a, k, at.yn, 1, 4, at.yn).wait_recv()
        if k % 2 == 1:
            far(a, k).start()
        copy(a, k, at.yn, 4, 5, at.sib).start()

    def forward_last(a, k):
        copy(a, k, at.diag, 5, 6, at.xn).wait_recv()
        copy(a, k, at.diag, 6, 7, at.sib).start()

    def load(a, k):
        buf = tok_buf if a == 0 else grad_buf
        return pltpu.make_async_copy(pairs[a][1].at[at.source(k)], buf, load_sem.at[a])

    def finish(a, k):
        copy(a, k, at.sib, 2, 1, at.sib).wait_recv()
        copy(a, k, at.xn + at.off_sib, 3, 3, at.sib).wait_recv()
        copy(a, k, at.yn + at.off_sib, 4, 5, at.sib).wait_recv()
        copy(a, k, at.diag + at.off_sib, 6, 7, at.sib).wait_recv()
        load(a, k).start()

    def raise_rows(k):
        mine = lax.broadcasted_iota(jnp.int32, gate.shape[1:], 1) == d
        held = jnp.where(mine, tok_buf[:, features:].astype(jnp.float32), 0.0)
        gate[k] = jnp.broadcast_to(jnp.sum(held, axis=1, keepdims=True), gate.shape[1:])

        @pl.loop(0, hidden // tile)
        def _(n):
            cols = pl.ds(pl.multiple_of(n * tile, tile), tile)
            raised[k, :, cols] = jnp.dot(
                tok_buf[:, :features], up[:, cols], preferred_element_type=jnp.float32
            )

    def lower_rows(k):
        total[...] = jnp.zeros_like(total)

        @pl.loop(0, hidden // tile)
        def _(n):
            cols = pl.ds(pl.multiple_of(n * tile, tile), tile)
            backward = lax.dot_general(
                grad_buf[...], down[cols, :], (((1,), (1,)), ((), ())),
                preferred_element_type=jnp.float32,
            )
            value = raised[k, :, cols]
            sig = jax.nn.sigmoid(value)
            terms = value * sig * backward
            total[...] += terms[:, :128] + terms[:, 128:]
            slope = sig * (1.0 + value * (1.0 - sig))
            inner[at.source(k), :, cols] = (gate[k][:, :1] * backward * slope).astype(
                jnp.bfloat16
            )

        mine = lax.broadcasted_iota(jnp.int32, total.shape, 1) == d
        summed = jnp.sum(total[...], axis=1, keepdims=True)
        gate_out[at.source(k)] = jnp.where(mine, summed, 0.0).astype(jnp.bfloat16)

    def compute(a, k):
        load(a, k).wait()
        if (a, k) == order[0]:
            up_load.wait()
        if (a, k) == order[1]:
            down_load.wait()
        if a == 0:
            raise_rows(k)
        else:
            lower_rows(k)

    order = [(0, 0), (1, 0), (0, 1), (0, 2), (0, 3), (1, 1), (1, 2), (1, 3)]
    steps = len(order)
    for a in range(2):
        local(a).start()
    for k in range(1, GROUPS):
        zcopy(0, k).start()
    for i in range(steps + 2):
        if i < steps:
            own(*order[i])
        if i == 1:
            for k in range(1, GROUPS):
                zcopy(1, k).start()
            up_load.start()
            down_load.start()
        if 1 <= i <= steps:
            forward(*order[i - 1])
        if i >= 2:
            forward_last(*order[i - 2])
            finish(*order[i - 2])
            compute(*order[i - 2])
    for a, k in order:
        copy(a, k, d, 0, 2, at.xn).wait_send()
        copy(a, k, d, 1, 4, at.yn).wait_send()
        copy(a, k, d, 2, 1, at.sib).wait_send()
        copy(a, k, at.xn, 3, 3, at.sib).wait_send()
        copy(a, k, at.yn, 4, 5, at.sib).wait_send()
        far(a, k).wait_send()
        copy(a, k, at.diag, 6, 7, at.sib).wait_send()
        if k:
            zcopy(a, k).wait_send()


def dispatch(tok, grad, up_matrix, down_matrix):
    groups, rows, wide = tok.shape
    features, hidden = up_matrix.shape
    lines = PEERS * rows
    anywhere = pl.BlockSpec(memory_space=pl.ANY)
    whole = pl.BlockSpec(memory_space=pltpu.VMEM)
    return pl.pallas_call(
        functools.partial(dispatch_kernel, rows),
        out_shape=(
            jax.ShapeDtypeStruct((groups, lines, wide), jnp.bfloat16),
            jax.ShapeDtypeStruct((groups, lines, features), jnp.bfloat16),
            jax.ShapeDtypeStruct((groups, lines, hidden), jnp.bfloat16),
            jax.ShapeDtypeStruct((groups, lines, LANES), jnp.bfloat16),
        ),
        in_specs=[anywhere] * 4,
        out_specs=(anywhere, anywhere, whole, whole),
        scratch_shapes=[
            pltpu.VMEM((features, hidden), jnp.bfloat16),
            pltpu.VMEM((hidden, features), jnp.bfloat16),
            pltpu.VMEM((lines, wide), jnp.bfloat16),
            pltpu.VMEM((lines, features), jnp.bfloat16),
            pltpu.VMEM((groups, lines, hidden), jnp.float32),
            pltpu.VMEM((groups, lines, LANES), jnp.float32),
            pltpu.VMEM((lines, LANES), jnp.float32),
            pltpu.SemaphoreType.DMA((2,)),
            pltpu.SemaphoreType.DMA((2,)),
            pltpu.SemaphoreType.DMA((2,)),
            pltpu.SemaphoreType.DMA((2, GROUPS)),
            pltpu.SemaphoreType.DMA((2, GROUPS)),
            pltpu.SemaphoreType.DMA((2, GROUPS, 7)),
            pltpu.SemaphoreType.DMA((2, GROUPS, 8)),
        ],
        compiler_params=pltpu.CompilerParams(
            collective_id=0, has_side_effects=True, vmem_limit_bytes=58 * MIB
        ),
    )(tok, grad, up_matrix, down_matrix)


def combine_kernel(
    rows, inner, gates, up, out, part, sib, dbuf, xbuf, ybuf, local_sem, zs, zr, ss, rs, ps, pr
):
    at = Place()
    g, d = at.group, at.dev
    features = up.shape[0]
    tile = 512
    at.barrier()

    def product(k):
        lines = inner[at.source(k)]

        @pl.loop(0, features // tile)
        def _(n):
            cols = pl.ds(pl.multiple_of(n * tile, tile), tile)
            block = lax.dot_general(
                lines, up[cols, :], (((1,), (1,)), ((), ())),
                preferred_element_type=jnp.float32,
            ).astype(jnp.bfloat16)
            part[k, :, :, cols] = block.reshape(PEERS, rows, tile)

        part[k, :, :, features:] = gates[at.source(k)].reshape(PEERS, rows, LANES)

    chips = (at.dev, at.xn, at.yn, at.diag)

    def pair(k, i):
        return pltpu.make_async_remote_copy(
            src_ref=part.at[k, chips[i] + at.off_sib], dst_ref=sib.at[k, i],
            send_sem=ps.at[k, i], recv_sem=pr.at[k, i],
            device_id=(g, at.sib), device_id_type=MESH,
        )

    def to(k, slot, origin, buf, peer):
        return pltpu.make_async_remote_copy(
            src_ref=part.at[k, origin], dst_ref=buf.at[k],
            send_sem=ss.at[k, slot], recv_sem=rs.at[k, slot],
            device_id=(g, peer), device_id_type=MESH,
        )

    def to_x(k):
        return to(k, 0, at.xn, xbuf, at.xn)

    def to_y(k):
        return to(k, 1, at.yn, ybuf, at.yn)

    def to_far(k):
        return to(k, 2, at.diag, dbuf, at.xn if k % 2 == 0 else at.yn)

    def add(k, origin, *terms):
        @pl.loop(0, rows // 16)
        def _(r):
            lines = pl.ds(pl.multiple_of(r * 16, 16), 16)
            total = part[k, origin, lines, :].astype(jnp.float32)
            for buf, index in terms:
                total = total + buf[index + (lines,)].astype(jnp.float32)
            part[k, origin, lines, :] = total.astype(jnp.bfloat16)

    def start_pairs(k):
        for i in (3, 1, 2, 0):
            pair(k, i).start()

    def first(k):
        for i in (3, 1, 2, 0):
            pair(k, i).wait_recv()
            if i == 3:
                add(k, at.diag, (sib, (k, 3)))
                to_far(k).start()
            elif i == 1:
                add(k, at.xn, (sib, (k, 1)))
                if k % 2 == 0:
                    to_x(k).start()
            elif i == 2:
                add(k, at.yn, (sib, (k, 2)))
                if k % 2 == 1:
                    to_y(k).start()

    def second(k):
        to_far(k).wait_recv()
        if k % 2 == 0:
            add(k, at.yn, (dbuf, (k,)))
            to_y(k).start()
        else:
            add(k, at.xn, (dbuf, (k,)))
            to_x(k).start()

    def home(k):
        target = at.source(k)
        return pltpu.make_async_remote_copy(
            src_ref=part.at[k, d], dst_ref=out.at[g],
            send_sem=zs.at[k], recv_sem=zr.at[k],
            device_id=(target, d), device_id_type=MESH,
        )

    def local():
        return pltpu.make_async_copy(part.at[0, d], out.at[g], local_sem)

    def third(k):
        to_x(k).wait_recv()
        to_y(k).wait_recv()
        add(k, d, (sib, (k, 0)), (xbuf, (k,)), (ybuf, (k,)))
        if k:
            home(k).start()
        else:
            local().start()

    order = (2, 1, 3, 0)
    for i in range(len(order) + 2):
        if i < len(order):
            product(order[i])
            start_pairs(order[i])
            first(order[i])
        if 1 <= i <= len(order):
            second(order[i - 1])
        if i >= 2:
            third(order[i - 2])
    for k in order:
        for i in range(4):
            pair(k, i).wait_send()
        to_x(k).wait_send()
        to_y(k).wait_send()
        to_far(k).wait_send()
        if k:
            home(k).wait_send()
            home(k).wait_recv()
    local().wait()


def combine(inner, gates, up_matrix, rows):
    wide = up_matrix.shape[0] + LANES
    whole = pl.BlockSpec(memory_space=pltpu.VMEM)
    hop = pltpu.VMEM((GROUPS, rows, wide), jnp.bfloat16)
    return pl.pallas_call(
        functools.partial(combine_kernel, rows),
        out_shape=jax.ShapeDtypeStruct((GROUPS, rows, wide), jnp.bfloat16),
        in_specs=[whole, whole, whole],
        out_specs=pl.BlockSpec(memory_space=pl.ANY),
        scratch_shapes=[
            pltpu.VMEM((GROUPS, PEERS, rows, wide), jnp.bfloat16),
            pltpu.VMEM((GROUPS, 4, rows, wide), jnp.bfloat16),
            hop,
            hop,
            hop,
            pltpu.SemaphoreType.DMA,
            pltpu.SemaphoreType.DMA((GROUPS,)),
            pltpu.SemaphoreType.DMA((GROUPS,)),
            pltpu.SemaphoreType.DMA((GROUPS, 3)),
            pltpu.SemaphoreType.DMA((GROUPS, 3)),
            pltpu.SemaphoreType.DMA((GROUPS, 4)),
            pltpu.SemaphoreType.DMA((GROUPS, 4)),
        ],
        compiler_params=pltpu.CompilerParams(
            collective_id=1, has_side_effects=True, vmem_limit_bytes=58 * MIB
        ),
    )(inner, gates, up_matrix)


def grouped(tokens, out_grad, gate_weights, expert_ids, slot_ids, up_weight, down_weight):
    rows_dev, features = tokens.shape
    experts = GROUPS * PEERS
    rows = 5 * rows_dev // 8
    up_matrix = up_weight[0]
    down_matrix = down_weight[0]
    names = expert_ids[:, :, None] == jnp.arange(experts, dtype=jnp.int32)
    in_group = jnp.any(
        (expert_ids // PEERS)[:, :, None] == jnp.arange(GROUPS, dtype=jnp.int32), axis=1
    )
    before = jnp.arange(rows_dev)[:, None] > jnp.arange(rows_dev)[None, :]
    rank = jnp.dot(
        before.astype(jnp.bfloat16), in_group.astype(jnp.bfloat16),
        preferred_element_type=jnp.float32,
    ).astype(jnp.int32)
    pick = jnp.logical_and(
        in_group[:, :, None],
        rank[:, :, None] == jnp.arange(rows, dtype=jnp.int32),
    ).astype(jnp.bfloat16)

    def packed(values):
        return jnp.einsum(
            "tgp,td->gpd", pick, values, preferred_element_type=jnp.float32
        ).astype(jnp.bfloat16)

    gate_table = jnp.sum(
        jnp.where(names, gate_weights.astype(jnp.float32)[:, :, None], 0.0), axis=1
    ).astype(jnp.bfloat16)
    gate_lanes = jnp.pad(
        gate_table.reshape(rows_dev, GROUPS, PEERS), ((0, 0), (0, 0), (0, LANES - PEERS))
    )
    gate_send = jnp.einsum(
        "tgp,tge->gpe", pick, gate_lanes, preferred_element_type=jnp.float32
    ).astype(jnp.bfloat16)
    inner, gates = dispatch(
        jnp.concatenate([packed(tokens), gate_send], axis=2),
        packed(out_grad),
        up_matrix,
        down_matrix,
    )[2:]
    halves = combine(inner, gates, up_matrix, rows)
    gate_tokens = jnp.einsum(
        "tgp,gpe->tge", pick, halves[:, :, features : features + PEERS],
        preferred_element_type=jnp.float32,
    ).reshape(rows_dev, experts)
    gate_grad = jnp.sum(jnp.where(names, gate_tokens[:, None, :], 0.0), axis=2).astype(
        jnp.bfloat16
    )
    token_grad = jnp.einsum(
        "tgp,gpd->td", pick, halves[:, :, :features], preferred_element_type=jnp.float32
    ).astype(jnp.bfloat16)
    return (token_grad, gate_grad)


def shards(tokens, out_grad, gate_weights, expert_ids, slot_ids, up_weight, down_weight):
    rows_dev = tokens.shape[0]
    features = tokens.shape[1]
    groups = lax.axis_size("group")
    per_group = lax.axis_size("dev")
    experts = groups * per_group
    capacity = 5 * rows_dev * TOPK // (4 * experts)
    slots_all = experts * capacity
    entries = rows_dev * TOPK
    up_matrix = up_weight[0]
    down_matrix = down_weight[0]
    group_of = expert_ids // per_group
    zero_row = jnp.zeros((1, features), jnp.bfloat16)
    token_pad = jnp.concatenate([tokens, zero_row])
    grad_pad = jnp.concatenate([out_grad, zero_row])
    gate_flat = jnp.concatenate([gate_weights.reshape(-1), jnp.zeros((1,), jnp.bfloat16)])
    target = (expert_ids * capacity + slot_ids).reshape(-1)
    slot_table = (
        jnp.full((slots_all,), entries, jnp.int32)
        .at[target]
        .set(jnp.arange(entries, dtype=jnp.int32))
    )
    anchor = slot_table // TOPK
    arrived = (
        lax.all_to_all(
            token_pad[anchor].reshape(experts, capacity, features),
            ("group", "dev"),
            split_axis=0,
            concat_axis=0,
            tiled=True,
        ),
        lax.all_to_all(
            grad_pad[anchor].reshape(experts, capacity, features),
            ("group", "dev"),
            split_axis=0,
            concat_axis=0,
            tiled=True,
        ),
        lax.all_to_all(
            gate_flat[slot_table].reshape(experts, capacity),
            ("group", "dev"),
            split_axis=0,
            concat_axis=0,
            tiled=True,
        ),
    )
    contrib, gate_rows = expert_rows(
        arrived[0].reshape(slots_all, features),
        arrived[1].reshape(slots_all, features),
        arrived[2].reshape(slots_all),
        up_matrix,
        down_matrix,
    )
    returned_rows = (
        lax.all_to_all(
            contrib.reshape(experts, capacity, features),
            ("group", "dev"),
            split_axis=0,
            concat_axis=0,
            tiled=True,
        ),
        lax.all_to_all(
            gate_rows.reshape(experts, capacity),
            ("group", "dev"),
            split_axis=0,
            concat_axis=0,
            tiled=True,
        ),
    )
    gathered = (
        returned_rows[0].reshape(slots_all, features)[target].reshape(rows_dev, TOPK, features)
    )
    gate_grad = returned_rows[1].reshape(-1)[target].reshape(rows_dev, TOPK)
    same_group = group_of == group_of[:, :1]
    selector = jnp.stack([same_group, jnp.logical_not(same_group)], axis=1).astype(jnp.bfloat16)
    halves = jnp.einsum(
        "tpk,tkd->tpd", selector, gathered, preferred_element_type=jnp.float32
    ).astype(jnp.bfloat16)
    token_grad = jnp.sum(halves.astype(jnp.float32), axis=1).astype(jnp.bfloat16)
    return (token_grad, gate_grad)


def solution(mesh):
    in_specs = (
        P(("group", "dev"), None),
        P(("group", "dev"), None),
        P(("group", "dev"), None),
        P(("group", "dev"), None),
        P(("group", "dev"), None),
        P(("group", "dev"), None, None),
        P(("group", "dev"), None, None),
    )
    out_specs = (P(("group", "dev"), None), P(("group", "dev"), None))
    fits = mesh.shape["group"] == GROUPS and mesh.shape["dev"] == PEERS
    step = grouped if fits else shards
    return jax.shard_map(step, mesh=mesh, in_specs=in_specs, out_specs=out_specs, check_vma=False)
```
